32 devices in a mesh: groups: 2 (over y), ctx: 4 (over x, core), shard: 4 (over z).
Axes of the slice: x: 2, y: 2, z: 4, core: 2. Of those that a mesh axis runs over, the one named last changes fastest.
Arguments:
- tokens: bfloat16 [2048, 8192], P(('groups', 'ctx'), 'shard'), parts along dimension 0, as said below
- gain: bfloat16 [8192], P('shard'), may hold values from 0.099609375 to 1.8984375
- w_query: bfloat16 [8192, 4096], P('ctx', 'shard'), may hold values from -0.0625 to 0.0625
- w_key: bfloat16 [1280, 4096], P('ctx', 'shard'), may hold values from -0.15625 to 0.15625
- w_value: bfloat16 [1280, 4096], P('ctx', 'shard'), may hold values from -0.15625 to 0.15625
- w_out: bfloat16 [4096, 8192], P('shard', 'ctx'), may hold values from -0.125 to 0.125
- latents: bfloat16 [2048, 1280], P(('groups', 'ctx')), parts along dimension 0, as said below
- image_pos: int32 [32], P(('groups', 'ctx')), parts along dimension 0, may hold values from -1 to 1023, as said below
- doc_lengths: int32 [12], P('groups'), parts along dimension 0, may hold values from 1 to 512, 1024 in all
- alpha: float32 [1], replicated, as said below
Outputs:
- mixed: bfloat16 [2048, 8192], P(('groups', 'ctx'), 'shard'), parts along dimension 0
The draws below stay inside these ranges and needn't reach their ends.
There are 2 independent parts, one for each index of `groups`. The reference program is written for one: setup_inputs(seed, part) draws one part's arguments, and reference() takes and returns one part's arrays. A program takes and returns all parts, laid end to end along the dimension named above; an argument that names none is the same for every part. Nothing has to cross between parts.
Inputs may be any that keep to these rules, and one draw needn't show every extreme that they name: `image_pos`: slot c * 4 + k (k below 4) is either empty (-1) or holds a position from c * 256 + k * 64 to c * 256 + (k + 1) * 64 - 1; slot 0 is always empty and the last slot always holds position 1023; another slot is used with probability about 0.3, so runs of token blocks carry no image of their own. `latents`: entries lie within -170 to 170. `tokens`: entries lie within -22 to 22. `alpha`: the magnitude lies within 0.6 to 2.0, of either sign.
All inputs are finite; a program needn't handle non-finite values.
Results may differ from the reference program's by a relative error of at most 0.015.
Values may be sent and summed in bfloat16 or wider, within the bound.
A program may use at most 192 MiB of HBM per device.

```python
import math
import jax
import jax.numpy as jnp
import numpy as np
from jax import lax

D = 8192
HEADS = 32
HEAD_DIM = 128
VD = 1280
LAT = 64
TOK_DEV = 256
SLOTS = 4
NDOCS = 6
TOKENS = 1024
IMAGES = 16
INNER = 4096
N_CTX = 4
N_SHARD = 4


def draw_tokens(key, part):
    key = jax.random.fold_in(key, 11)
    key_scale, key_base = jax.random.split(key, 2)
    col_scale = jnp.exp(jax.random.uniform(key_scale, (D,), jnp.float32, jnp.log(0.32), jnp.log(3.2)))
    base_draw = jnp.clip(jax.random.normal(key_base, (TOKENS, D), jnp.float32), -6.0, 6.0)
    return jnp.clip(base_draw * col_scale[None, :], -22.0, 22.0).astype(jnp.bfloat16)


def draw_latents(key, part):
    key = jax.random.fold_in(key, 12)
    key_base = jax.random.fold_in(key, 0)
    total_rows = IMAGES * LAT
    whole_draw = jnp.clip(jax.random.normal(key_base, (total_rows, VD), jnp.float32), -6.0, 6.0)
    return jnp.clip(whole_draw, -170.0, 170.0).astype(jnp.bfloat16)


def draw_image_pos(key, part):
    key = jax.random.fold_in(key, 13)
    key_offset, key_used = jax.random.split(key)
    block_count = IMAGES // SLOTS
    span = TOK_DEV // SLOTS
    offset = jax.random.randint(key_offset, (block_count, SLOTS), 0, span) + jnp.arange(SLOTS, dtype=jnp.int32)[None, :] * span
    block_base = jnp.arange(block_count, dtype=jnp.int32)[:, None] * TOK_DEV
    used_slot = jax.random.randint(key_used, (block_count, SLOTS), 0, 10) < 3
    placed = jnp.where(used_slot, block_base + offset, -1).astype(jnp.int32).reshape(IMAGES)
    placed = placed.at[0].set(jnp.int32(-1))
    placed = placed.at[IMAGES - 1].set(jnp.int32(TOKENS - 1))
    return placed.astype(jnp.int32)


def draw_alpha(key, part):
    key = jax.random.fold_in(key, 14)
    key_sign, key_size = jax.random.split(key)
    sign_bit = jax.random.randint(key_sign, (1,), 0, 2)
    sign_value = 2.0 * sign_bit.astype(jnp.float32) - 1.0
    magnitude = jnp.exp(jax.random.uniform(key_size, (1,), jnp.float32, jnp.log(0.6), jnp.log(2.0)))
    return (sign_value * magnitude).astype(jnp.float32)


def raised(entries, rng, source, target, blocks, factor):
    def block_of(dim):
        return (jnp.arange(entries.shape[dim]) // (entries.shape[dim] // blocks)).reshape((-1,) + (1,) * (entries.ndim - 1 - dim))

    first = jax.random.permutation(rng, blocks)[block_of(target)]
    far = (block_of(target) + blocks // 2) % blocks
    return jnp.where((block_of(source) == first) | (block_of(source) == far), factor * entries, entries)


def level_of(stream_key, extent, shards, least, high):
    def one(dim, shards_of):
        draws = jax.random.uniform(jax.random.fold_in(jax.random.fold_in(stream_key, 6), dim), (shards_of,), jnp.float32, least / len(shards), high / len(shards))
        return jnp.repeat(jnp.exp(draws), extent[dim] // shards_of).reshape((-1,) + (1,) * (len(extent) - dim - 1))

    factor_of = one(*shards[0])
    for cut in shards[1:]:
        factor_of = factor_of * one(*cut)
    return factor_of


def split_up(count, total, bound, lean):
    portions = [(1 << 20) // math.isqrt(grade ** lean) + 1 for grade in range(2, count + 1)]
    spare, given = total - bound - (count - 1), [1] * (count - 1)
    while spare > 0:
        candidates = [i for i in range(count - 1) if given[i] < bound]
        mass, left = sum([portions[i] for i in candidates]), spare
        for i in candidates:
            more = min(bound - given[i], max(1, left * portions[i] // mass), spare)
            given[i] = given[i] + more
            spare = spare - more
    return np.array([bound] + given)


def ragged(rng, number_of, total, bound, lean):
    if number_of == 2:
        one = jax.random.randint(rng, (), max(1, total - bound), min(bound, total - 1) + 1)
        return jnp.stack([one, total - one])
    lengths = jnp.asarray(split_up(number_of, total, bound, lean), jnp.int32)
    couples = (number_of - 1) // 2
    source_of, taker = lengths[1:1 + 2 * couples:2], lengths[2:2 + 2 * couples:2]
    slack = jnp.minimum(source_of - 1, bound - taker)
    passed = jax.random.randint(jax.random.fold_in(rng, 1), (couples,), 0, 1 << 20) % (slack + 1)
    lengths = lengths.at[1:1 + 2 * couples:2].set(source_of - passed).at[2:2 + 2 * couples:2].set(taker + passed)
    return lengths[jax.random.permutation(jax.random.fold_in(rng, 2), number_of)]


def centred(rng, dims, deviation, reach, pieces=(), kind=jnp.bfloat16):
    array = jax.random.normal(rng, dims, jnp.float32) * deviation
    if len(pieces) > 0:
        array = level_of(rng, dims, pieces, -0.22, 0.18) * array
    return jnp.clip(array, min=-reach, max=reach).astype(kind)


def noise_with(own_key, dims, scale, limit, cuts, heavy, held_as=jnp.bfloat16):
    values = scale * jax.random.normal(own_key, dims, jnp.float32)
    if cuts:
        values = values * level_of(own_key, dims, cuts, -0.22, 0.18)
    return jnp.clip(raised(values, jax.random.fold_in(own_key, 3), *heavy), -limit, limit).astype(held_as)


def setup_inputs(seed: int = 0, part: int = 0) -> dict:
    key_of = jax.random.split(jax.random.key(seed), 11)
    own_keys = jax.random.split(jax.random.fold_in(key_of[10], part), 11)
    return {
        "tokens": draw_tokens(jax.random.fold_in(jax.random.fold_in(key_of[10], part), 71), part),
        "gain": jnp.clip(1.0 + 0.18 * jax.random.normal(key_of[1], (D,), jnp.float32), 0.099609375, 1.8984375).astype(jnp.bfloat16),
        "w_query": centred(key_of[2], (D, INNER), D ** -0.5, 0.0625, ((0, 4), (1, 4))),
        "w_key": centred(key_of[3], (VD, INNER), VD ** -0.5, 0.15625, ((0, 4), (1, 4))),
        "w_value": centred(key_of[4], (VD, INNER), VD ** -0.5, 0.15625, ((0, 4), (1, 4))),
        "w_out": noise_with(key_of[5], (INNER, D), INNER ** -0.5, 0.125, ((0, 4), (1, 4)), (0, 1, 4, 2.0)),
        "latents": draw_latents(jax.random.fold_in(jax.random.fold_in(key_of[10], part), 71), part),
        "image_pos": draw_image_pos(jax.random.fold_in(jax.random.fold_in(key_of[10], part), 71), part),
        "doc_lengths": ragged(own_keys[8], NDOCS, TOKENS, TOKENS // 2, 2).astype(jnp.int32),
        "alpha": draw_alpha(jax.random.fold_in(key_of[10], 71), part),
    }


def reference(tokens, gain, w_query, w_key, w_value, w_out, latents, image_pos, doc_lengths, alpha):
    widened = tokens.astype(jnp.float32)
    mean_square = lax.optimization_barrier(jnp.mean(widened * widened, axis=-1, keepdims=True))
    normed = (widened * lax.rsqrt(mean_square + 1e-06) * gain.astype(jnp.float32)).astype(jnp.bfloat16)
    queries = jnp.dot(normed, w_query, preferred_element_type=jnp.float32).astype(jnp.bfloat16)
    key_rows = jnp.dot(latents, w_key, preferred_element_type=jnp.float32).astype(jnp.bfloat16)
    value_rows = jnp.dot(latents, w_value, preferred_element_type=jnp.float32).astype(jnp.bfloat16)
    position = jnp.arange(TOKENS, dtype=jnp.int32)
    slot_ids = jnp.arange(IMAGES, dtype=jnp.int32)
    eligible = (image_pos[None, :] >= 0) & (image_pos[None, :] <= position[:, None])
    chosen = lax.optimization_barrier(jnp.max(jnp.where(eligible, slot_ids[None, :], -1), axis=1))
    chosen_pos = lax.optimization_barrier(jnp.max(jnp.where(eligible, image_pos[None, :], -1), axis=1))
    starts = jnp.cumsum(doc_lengths) - doc_lengths
    doc_start = lax.optimization_barrier(jnp.max(jnp.where(starts[None, :] <= position[:, None], starts[None, :], 0), axis=1))
    gate_open = (chosen >= 0) & (chosen_pos >= doc_start)
    latent_image = jnp.arange(IMAGES * LAT, dtype=jnp.int32) // LAT
    key_heads = key_rows.astype(jnp.float32).reshape(IMAGES * LAT, HEADS, HEAD_DIM)
    value_heads = value_rows.astype(jnp.float32).reshape(IMAGES * LAT, HEADS, HEAD_DIM)
    score_scale = 1.0 / HEAD_DIM ** 0.5

    def attend_block(packed):
        block_query, block_chosen = packed
        query_heads = block_query.astype(jnp.float32).reshape(TOK_DEV, HEADS, HEAD_DIM)
        scores = jnp.einsum('thd,khd->htk', query_heads, key_heads) * score_scale
        allowed = latent_image[None, :] == block_chosen[:, None]
        scores = jnp.where(allowed[None, :, :], scores, jnp.float32(-1e+30))
        probs = jax.nn.softmax(scores, axis=-1).astype(jnp.bfloat16)
        result = jnp.einsum('htk,khd->thd', probs.astype(jnp.float32), value_heads)
        return result.reshape(TOK_DEV, INNER).astype(jnp.bfloat16)
    attended = lax.map(attend_block, (queries.reshape(N_CTX, TOK_DEV, INNER), chosen.reshape(N_CTX, TOK_DEV)))
    attended = attended.reshape(TOKENS, INNER)
    group_width = INNER // N_SHARD
    branch = jnp.zeros((TOKENS, D), jnp.float32)
    for group in range(N_SHARD):
        partial_sum = jnp.dot(attended[:, group * group_width:(group + 1) * group_width], w_out[group * group_width:(group + 1) * group_width], preferred_element_type=jnp.float32).astype(jnp.bfloat16)
        partial_sum = lax.optimization_barrier(partial_sum)
        branch = branch + partial_sum.astype(jnp.float32)
    factor = jnp.tanh(alpha[0]) * gate_open.astype(jnp.float32)
    return (widened + factor[:, None] * branch).astype(jnp.bfloat16)
```

```python
import jax
import jax.numpy as jnp
from jax import lax
from jax.sharding import PartitionSpec as P

HEAD_DIM = 128


FLIP_FAR = [(0, 2), (1, 3), (2, 0), (3, 1)]
FLIP_NEAR = [(0, 1), (1, 0), (2, 3), (3, 2)]
FLIP_GROUP = [(0, 1), (1, 0)]


def gathered_panels(panel, chunks):
    mine, group = lax.axis_index("ctx"), lax.axis_index("groups")
    half = panel.shape[0] // 2
    size = half // chunks
    near_owner, far_owner, diagonal = mine ^ 1, mine ^ 2, mine ^ 3
    pieces = [(mine, 0, panel), (near_owner, 0, lax.ppermute(panel, "ctx", FLIP_NEAR))]
    for chunk in range(chunks):
        first = group * half + chunk * size
        other_first = (1 - group) * half + chunk * size
        sent = lax.dynamic_slice_in_dim(panel, first, size, 0)
        direct = lax.ppermute(sent, "ctx", FLIP_FAR)
        handed = lax.ppermute(direct, "groups", FLIP_GROUP)
        pieces.append((far_owner, first, direct))
        pieces.append((far_owner, other_first, handed))
        pieces.append((diagonal, first, lax.ppermute(direct, "ctx", FLIP_NEAR)))
        pieces.append((diagonal, other_first, lax.ppermute(handed, "ctx", FLIP_NEAR)))
    return pieces


def whole_panel(panel, axis_size, chunks=1):
    if axis_size != 4:
        return lax.all_gather(panel, "ctx", axis=0, tiled=True)
    rows = panel.shape[0]
    whole = jnp.zeros((rows * 4, panel.shape[1]), panel.dtype)
    for owner, first, part in gathered_panels(panel, chunks):
        whole = lax.dynamic_update_slice_in_dim(whole, part, owner * rows + first, 0)
    return whole


def project_in(normed, panel, axis_size):
    if axis_size != 4:
        whole = lax.all_gather(panel, "ctx", axis=0, tiled=True)
        return jnp.dot(normed, whole, preferred_element_type=jnp.float32)
    total = 0.0
    for owner, first, part in gathered_panels(panel, 2):
        start = owner * panel.shape[0] + first
        columns = lax.dynamic_slice_in_dim(normed, start, part.shape[0], 1)
        total = total + jnp.dot(columns, part, preferred_element_type=jnp.float32)
    return total


def project_out(attended, panel, axis_size):
    if axis_size != 4:
        whole = lax.all_gather(panel, "ctx", axis=1, tiled=True)
        return jnp.dot(attended, whole, preferred_element_type=jnp.float32).astype(jnp.bfloat16)
    width = panel.shape[1]
    whole = jnp.zeros((attended.shape[0], 4 * width), jnp.bfloat16)
    by_owner = {}
    for place, (owner, first, part) in enumerate(gathered_panels(panel, 2)):
        key = place if place < 2 else 2 + (place - 2) % 4 // 2
        by_owner.setdefault(key, []).append((owner, first, part))
    for parts in by_owner.values():
        total = 0.0
        for owner, first, part in parts:
            rows = lax.dynamic_slice_in_dim(attended, first, part.shape[0], 1)
            total = total + jnp.dot(rows, part, preferred_element_type=jnp.float32)
        whole = lax.dynamic_update_slice_in_dim(
            whole, total.astype(jnp.bfloat16), parts[0][0] * width, 1
        )
    return whole


def latest_before(image_pos, latents, lat_rows):
    count, mine = lax.axis_size("ctx"), lax.axis_index("ctx")
    slot_ids = jnp.arange(image_pos.shape[0], dtype=jnp.int32)
    used = image_pos >= 0
    last_slot = jnp.maximum(jnp.max(jnp.where(used, slot_ids, -1)), 0)
    last_pos = jnp.max(jnp.where(used, image_pos, -1))
    last_rows = lax.dynamic_slice_in_dim(latents, last_slot * lat_rows, lat_rows, 0)
    column = jnp.arange(latents.shape[1], dtype=jnp.int32)[None, :]
    digits = jnp.where(column == 0, last_pos // 64, jnp.where(column == 1, last_pos % 64, 0))
    tag = jnp.broadcast_to(digits, (16, latents.shape[1])).astype(jnp.bfloat16)
    blocks = lax.all_gather(jnp.concatenate([last_rows, tag], axis=0), "ctx")
    places = blocks[:, lat_rows, :2].astype(jnp.int32)
    places = places[:, 0] * 64 + places[:, 1]
    before = jnp.arange(count, dtype=jnp.int32) < mine
    pos = jnp.max(jnp.where(before, places, -1))
    source = jnp.argmax(jnp.where(before, places, -1))
    rows = lax.dynamic_index_in_dim(blocks, source, 0, keepdims=False)[:lat_rows]
    return pos, rows


def body(tokens, gain, w_query, w_key, w_value, w_out, latents, image_pos, doc_lengths, alpha):
    n_ctx = lax.axis_size("ctx")
    tok_rows = tokens.shape[0]
    slot_count = image_pos.shape[0]
    lat_rows = latents.shape[0] // slot_count
    carried_pos, carried_rows = latest_before(image_pos, latents, lat_rows)
    gathered = lax.all_gather(tokens, "shard", axis=1, tiled=True)
    full_gain = lax.all_gather(gain, "shard", axis=0, tiled=True)
    widened = gathered.astype(jnp.float32)
    mean_square = jnp.mean(widened * widened, axis=-1, keepdims=True)
    normed = (widened * lax.rsqrt(mean_square + 1e-06) * full_gain.astype(jnp.float32)).astype(
        jnp.bfloat16
    )
    kv_panel = whole_panel(jnp.concatenate([w_key, w_value], axis=1), n_ctx)
    all_latents = jnp.concatenate([carried_rows, latents], axis=0)
    all_kv = jnp.dot(all_latents, kv_panel, preferred_element_type=jnp.float32).astype(jnp.bfloat16)
    all_keys, all_values = jnp.split(all_kv, 2, axis=1)
    queries = project_in(normed, w_query, n_ctx).astype(jnp.bfloat16)
    cand_pos = jnp.concatenate([jnp.reshape(carried_pos, (1,)), image_pos]).astype(jnp.int32)
    cand_ids = jnp.arange(slot_count + 1, dtype=jnp.int32)
    position = lax.axis_index("ctx") * tok_rows + jnp.arange(tok_rows, dtype=jnp.int32)
    eligible = (cand_pos[None, :] >= 0) & (cand_pos[None, :] <= position[:, None])
    chosen = jnp.max(jnp.where(eligible, cand_ids[None, :], -1), axis=1)
    chosen_pos = jnp.max(jnp.where(eligible, cand_pos[None, :], -1), axis=1)
    starts = jnp.cumsum(doc_lengths) - doc_lengths
    doc_start = jnp.max(jnp.where(starts[None, :] <= position[:, None], starts[None, :], 0), axis=1)
    gate_open = (chosen >= 0) & (chosen_pos >= doc_start)
    latent_image = jnp.arange((slot_count + 1) * lat_rows, dtype=jnp.int32) // lat_rows
    head_count = queries.shape[1] // HEAD_DIM
    query_heads = queries.reshape(tok_rows, head_count, HEAD_DIM)
    key_heads = all_keys.reshape(all_keys.shape[0], head_count, HEAD_DIM)
    value_heads = all_values.reshape(all_values.shape[0], head_count, HEAD_DIM)
    score_scale = 1.0 / HEAD_DIM**0.5
    scores = (
        jnp.einsum("thd,khd->htk", query_heads, key_heads, preferred_element_type=jnp.float32)
        * score_scale
    )
    allowed = latent_image[None, :] == chosen[:, None]
    scores = jnp.where(allowed[None, :, :], scores, jnp.float32(-1e30))
    probs = jax.nn.softmax(scores, axis=-1).astype(jnp.bfloat16)
    attended = jnp.einsum("htk,khd->thd", probs, value_heads, preferred_element_type=jnp.float32)
    attended = attended.reshape(tok_rows, head_count * HEAD_DIM).astype(jnp.bfloat16)
    partial_terms = project_out(attended, w_out, n_ctx)
    branch = lax.psum_scatter(partial_terms, "shard", scatter_dimension=1, tiled=True).astype(
        jnp.float32
    )
    factor = jnp.tanh(alpha[0]) * gate_open.astype(jnp.float32)
    return (tokens.astype(jnp.float32) + factor[:, None] * branch).astype(jnp.bfloat16)


def solution(mesh):
    in_specs = (
        P(("groups", "ctx"), "shard"),
        P("shard"),
        P("ctx", "shard"),
        P("ctx", "shard"),
        P("ctx", "shard"),
        P("shard", "ctx"),
        P(("groups", "ctx"), None),
        P(("groups", "ctx")),
        P("groups"),
        P(),
    )
    out_specs = P(("groups", "ctx"), "shard")
    return jax.shard_map(body, mesh=mesh, in_specs=in_specs, out_specs=out_specs, check_vma=False)
```

```python
import functools

import jax
import jax.numpy as jnp
from jax import lax
from jax.experimental import pallas as pl
from jax.experimental.pallas import tpu as pltpu
from jax.sharding import PartitionSpec as P

HEAD_DIM = 128


def carried_in(value, axis, join, neutral):
    count, mine = (lax.axis_size(axis), lax.axis_index(axis))
    pieces = jax.tree.map(lambda part: lax.all_gather(part, axis), value)
    subtotal = jax.tree.map(
        lambda part, zero: jnp.full_like(part, 0) + jnp.asarray(zero, part.dtype), value, neutral
    )

    def lap(position, subtotal):
        longer = join(subtotal, jax.tree.map(lambda part: part[position], pieces))
        return jax.tree.map(lambda new, old: jnp.where(position < mine, new, old), longer, subtotal)

    return lax.fori_loop(0, count - 1, lap, subtotal)


def take_newer(before_part, after_part):
    newer_open = after_part[0] >= 0
    return tuple(
        (
            jnp.where(newer_open, after_item, before_item)
            for before_item, after_item in zip(before_part, after_part)
        )
    )


def plain_body(tokens, gain, w_query, w_key, w_value, w_out, latents, image_pos, doc_lengths, alpha):
    tok_rows = tokens.shape[0]
    gathered, full_gain = (
        lax.all_gather(tokens, "shard", axis=1, tiled=True),
        lax.all_gather(gain, "shard", axis=0, tiled=True),
    )
    widened = gathered.astype(jnp.float32)
    mean_square = jnp.mean(widened * widened, axis=-1, keepdims=True)
    normed = (widened * lax.rsqrt(mean_square + 1e-06) * full_gain.astype(jnp.float32)).astype(
        jnp.bfloat16
    )
    key_panel, value_panel = (
        lax.all_gather(w_key, "ctx", axis=0, tiled=True),
        lax.all_gather(w_value, "ctx", axis=0, tiled=True),
    )
    query_panel, out_panel = (
        lax.all_gather(w_query, "ctx", axis=0, tiled=True),
        lax.all_gather(w_out, "ctx", axis=1, tiled=True),
    )
    queries = jnp.dot(normed, query_panel, preferred_element_type=jnp.float32).astype(jnp.bfloat16)
    slot_count = image_pos.shape[0]
    lat_rows = latents.shape[0] // slot_count
    slot_ids = jnp.arange(slot_count, dtype=jnp.int32)
    slot_used = image_pos >= 0
    last_slot = jnp.maximum(jnp.max(jnp.where(slot_used, slot_ids, -1)), 0)
    last_pos = jnp.max(jnp.where(slot_used, image_pos, -1))
    local_keys = jnp.dot(latents, key_panel, preferred_element_type=jnp.float32).astype(
        jnp.bfloat16
    )
    local_values = jnp.dot(latents, value_panel, preferred_element_type=jnp.float32).astype(
        jnp.bfloat16
    )
    last_key = lax.dynamic_slice_in_dim(local_keys, last_slot * lat_rows, lat_rows, 0)
    last_value = lax.dynamic_slice_in_dim(local_values, last_slot * lat_rows, lat_rows, 0)
    identity = (jnp.int32(-1), jnp.zeros_like(last_key), jnp.zeros_like(last_value))
    carried_pos, carried_key, carried_value = carried_in(
        (last_pos, last_key, last_value), "ctx", take_newer, identity
    )
    all_keys = jnp.concatenate([carried_key, local_keys], axis=0)
    all_values = jnp.concatenate([carried_value, local_values], axis=0)
    cand_pos = jnp.concatenate([jnp.reshape(carried_pos, (1,)), image_pos]).astype(jnp.int32)
    cand_ids = jnp.arange(slot_count + 1, dtype=jnp.int32)
    position = lax.axis_index("ctx") * tok_rows + jnp.arange(tok_rows, dtype=jnp.int32)
    eligible = (cand_pos[None, :] >= 0) & (cand_pos[None, :] <= position[:, None])
    chosen = jnp.max(jnp.where(eligible, cand_ids[None, :], -1), axis=1)
    chosen_pos = jnp.max(jnp.where(eligible, cand_pos[None, :], -1), axis=1)
    starts = jnp.cumsum(doc_lengths) - doc_lengths
    doc_start = jnp.max(jnp.where(starts[None, :] <= position[:, None], starts[None, :], 0), axis=1)
    gate_open = (chosen >= 0) & (chosen_pos >= doc_start)
    latent_image = jnp.arange((slot_count + 1) * lat_rows, dtype=jnp.int32) // lat_rows
    head_count = queries.shape[1] // HEAD_DIM
    query_heads = queries.reshape(tok_rows, head_count, HEAD_DIM)
    key_heads = all_keys.reshape(all_keys.shape[0], head_count, HEAD_DIM)
    value_heads = all_values.reshape(all_values.shape[0], head_count, HEAD_DIM)
    score_scale = 1.0 / HEAD_DIM**0.5
    scores = (
        jnp.einsum("thd,khd->htk", query_heads, key_heads, preferred_element_type=jnp.float32)
        * score_scale
    )
    allowed = latent_image[None, :] == chosen[:, None]
    scores = jnp.where(allowed[None, :, :], scores, jnp.float32(-1e30))
    probs = jax.nn.softmax(scores, axis=-1).astype(jnp.bfloat16)
    attended = jnp.einsum("htk,khd->thd", probs, value_heads, preferred_element_type=jnp.float32)
    attended = attended.reshape(tok_rows, head_count * HEAD_DIM).astype(jnp.bfloat16)
    partial_terms = jnp.dot(attended, out_panel, preferred_element_type=jnp.float32)
    branch = lax.psum_scatter(
        partial_terms.astype(jnp.bfloat16), "shard", scatter_dimension=1, tiled=True
    ).astype(jnp.float32)
    factor = jnp.tanh(alpha[0]) * gate_open.astype(jnp.float32)
    return (tokens.astype(jnp.float32) + factor[:, None] * branch).astype(jnp.bfloat16)


MESH_ID = pl.DeviceIdType.MESH
F32, BF16 = jnp.float32, jnp.bfloat16

CARRY = 0
TOK_UP, TOK_DOWN = 3, 6
KV = 9
QUERY = 14
OUT = 23
SUM_UP, SUM_DOWN = 32, 36
TRANSFERS = 40
CHUNKS = 2


def kernel(
    slots,
    lat_rows,
    pos_ref,
    docs_ref,
    gate_ref,
    tok_in,
    tok_ref,
    wq_in,
    wkv_in,
    wout_in,
    carry_in,
    lat_ref,
    out_ref,
    tok,
    wq,
    wkv,
    wout,
    carry,
    lat_all,
    kv,
    qacc,
    att,
    part,
    up_buf,
    down_buf,
    send_sem,
    recv_sem,
    own_sem,
):
    group, mine, z = lax.axis_index("groups"), lax.axis_index("ctx"), lax.axis_index("shard")
    rows_t = tok_ref.shape[0]
    x, core = mine // 2, mine % 2
    near = x * 2 + 1 - core
    far = (1 - x) * 2 + core
    diagonal = (1 - x) * 2 + 1 - core

    def at(ctx=None, groups=None, shard=None):
        return (
            group if groups is None else groups,
            mine if ctx is None else ctx,
            z if shard is None else shard,
        )

    def copy(number, src, dst, device):
        return pltpu.make_async_remote_copy(
            src_ref=src,
            dst_ref=dst,
            send_sem=send_sem.at[number],
            recv_sem=recv_sem.at[number],
            device_id=device,
            device_id_type=MESH_ID,
        )

    barrier = pltpu.get_barrier_semaphore()
    for device in (at(ctx=near), at(ctx=far), at(ctx=diagonal), at(groups=1 - group)):
        pl.semaphore_signal(barrier, inc=1, device_id=device, device_id_type=MESH_ID)

    @pl.when(z > 0)
    def _():
        pl.semaphore_signal(barrier, inc=1, device_id=at(shard=z - 1), device_id_type=MESH_ID)

    @pl.when(z < 3)
    def _():
        pl.semaphore_signal(barrier, inc=1, device_id=at(shard=z + 1), device_id_type=MESH_ID)

    @pl.when((z > 0) & (z < 3))
    def _():
        pl.semaphore_wait(barrier, 6)

    @pl.when((z == 0) | (z == 3))
    def _():
        pl.semaphore_wait(barrier, 5)

    def tok_up(step):
        src = tok_in if step == 0 else tok.at[z - step]
        return copy(TOK_UP + step, src, tok.at[z - step], at(shard=z + 1))

    def tok_up_arrival(step):
        return copy(TOK_UP + step, tok.at[z - 1 - step], tok.at[z - 1 - step], at(shard=z + 1))

    def tok_down(step):
        src = tok_in if step == 0 else tok.at[z + step]
        return copy(TOK_DOWN + step, src, tok.at[z + step], at(shard=z - 1))

    def tok_down_arrival(step):
        return copy(TOK_DOWN + step, tok.at[z + 1 + step], tok.at[z + 1 + step], at(shard=z - 1))

    def start_tokens(step):
        @pl.when((z - step >= 0) & (z < 3))
        def _():
            tok_up(step).start()

        @pl.when((z + step <= 3) & (z > 0))
        def _():
            tok_down(step).start()

    def arrived_tokens(step):
        @pl.when(z - 1 - step >= 0)
        def _():
            tok_up_arrival(step).wait_recv()

        @pl.when(z + 1 + step <= 3)
        def _():
            tok_down_arrival(step).wait_recv()

    def sent_tokens(step):
        @pl.when((z - step >= 0) & (z < 3))
        def _():
            tok_up(step).wait_send()

        @pl.when((z + step <= 3) & (z > 0))
        def _():
            tok_down(step).wait_send()

    class Panels:
        def __init__(self, number, source, buffer, chunks):
            self.number, self.source, self.buffer = number, source, buffer
            self.rows = source.shape[0]
            self.half = self.rows // 2
            self.size = self.half // chunks
            self.chunks = chunks

        def piece(self, owner, first, size):
            return self.buffer.at[owner, pl.ds(first, size)]

        def first(self, which, chunk):
            return which * self.half + chunk * self.size

        def near(self):
            return copy(self.number, self.source, self.buffer.at[mine], at(ctx=near))

        def far(self, chunk):
            first = self.first(group, chunk)
            src = self.source.at[pl.ds(first, self.size)]
            dst = self.piece(mine, first, self.size)
            return copy(self.number + 1 + 4 * chunk, src, dst, at(ctx=far))

        def handed(self, chunk):
            ref = self.piece(far, self.first(group, chunk), self.size)
            return copy(self.number + 2 + 4 * chunk, ref, ref, at(groups=1 - group))

        def diagonal_far(self, chunk):
            ref = self.piece(far, self.first(group, chunk), self.size)
            return copy(self.number + 3 + 4 * chunk, ref, ref, at(ctx=near))

        def diagonal_handed(self, chunk):
            ref = self.piece(far, self.first(1 - group, chunk), self.size)
            return copy(self.number + 4 + 4 * chunk, ref, ref, at(ctx=near))

        def got_near(self):
            ref = self.buffer.at[near]
            copy(self.number, ref, ref, at(ctx=near)).wait_recv()

        def got_far(self, chunk):
            ref = self.piece(far, self.first(group, chunk), self.size)
            copy(self.number + 1 + 4 * chunk, ref, ref, at(ctx=far)).wait_recv()
            self.handed(chunk).start()
            self.diagonal_far(chunk).start()

        def got_handed(self, chunk):
            ref = self.piece(far, self.first(1 - group, chunk), self.size)
            copy(self.number + 2 + 4 * chunk, ref, ref, at(groups=1 - group)).wait_recv()
            self.diagonal_handed(chunk).start()

        def got_diagonal_far(self, chunk):
            ref = self.piece(diagonal, self.first(group, chunk), self.size)
            copy(self.number + 3 + 4 * chunk, ref, ref, at(ctx=near)).wait_recv()

        def got_diagonal_handed(self, chunk):
            ref = self.piece(diagonal, self.first(1 - group, chunk), self.size)
            copy(self.number + 4 + 4 * chunk, ref, ref, at(ctx=near)).wait_recv()

        def sent(self):
            self.near().wait_send()
            for chunk in range(self.chunks):
                self.far(chunk).wait_send()
                self.handed(chunk).wait_send()
                self.diagonal_far(chunk).wait_send()
                self.diagonal_handed(chunk).wait_send()

    kv_panels = Panels(KV, wkv_in, wkv, 1)
    q_panels = Panels(QUERY, wq_in, wq, CHUNKS)
    out_panels = Panels(OUT, wout_in, wout, CHUNKS)

    carries = [
        copy(CARRY + i, carry_in, carry.at[mine], at(ctx=peer))
        for i, peer in enumerate((near, far, diagonal))
    ]
    start_tokens(0)
    for sending in carries:
        sending.start()
    kv_panels.far(0).start()
    kv_panels.near().start()
    for chunk in range(CHUNKS):
        q_panels.far(chunk).start()
    q_panels.near().start()
    own = [
        pltpu.make_async_copy(wkv_in, wkv.at[mine], own_sem.at[0]),
        pltpu.make_async_copy(carry_in, carry.at[mine], own_sem.at[1]),
        pltpu.make_async_copy(tok_in, tok.at[z], own_sem.at[2]),
        pltpu.make_async_copy(wq_in, wq.at[mine], own_sem.at[3]),
        pltpu.make_async_copy(wout_in, wout.at[mine], own_sem.at[4]),
    ]
    for local in own:
        local.start()

    own[1].wait()
    for i, peer in enumerate((near, far, diagonal)):
        copy(CARRY + i, carry.at[peer], carry.at[peer], at(ctx=peer)).wait_recv()
    held_pos = jnp.full((1, 1), -1.0, F32)
    lat_all[pl.ds(0, lat_rows)] = jnp.zeros((lat_rows, lat_ref.shape[1]), BF16)
    for block in range(4):
        tag = carry[block, pl.ds(lat_rows, 16)].astype(F32)
        place = tag[0:1, 0:1] * 64.0 + tag[0:1, 1:2]
        newer = (place >= 0.0) & (block < mine)
        held_pos = jnp.where(newer, place, held_pos)
        lat_all[pl.ds(0, lat_rows)] = jnp.where(
            newer, carry[block, pl.ds(0, lat_rows)].astype(F32), lat_all[pl.ds(0, lat_rows)].astype(F32)
        ).astype(BF16)
    lat_all[pl.ds(lat_rows, slots * lat_rows)] = lat_ref[...]

    kv_panels.got_far(0)
    arrived_tokens(0)
    start_tokens(1)
    kv_panels.got_handed(0)
    q_panels.got_far(0)
    out_panels.near().start()
    arrived_tokens(1)
    start_tokens(2)

    own[0].wait()
    kv_panels.got_near()
    kv_panels.got_diagonal_far(0)
    kv_panels.got_diagonal_handed(0)
    depth = wkv.shape[1]
    tile = 512

    @pl.loop(0, wkv.shape[2] // tile)
    def _(step):
        columns = pl.ds(pl.multiple_of(step * tile, tile), tile)
        weight = wkv[:, :, columns].reshape(4 * depth, tile)
        kv[:, columns] = jnp.dot(lat_all[...], weight, preferred_element_type=F32).astype(BF16)

    q_panels.got_far(1)
    for chunk in range(CHUNKS):
        out_panels.far(chunk).start()
    q_panels.got_handed(0)
    arrived_tokens(2)
    own[2].wait()
    for step in range(3):
        sent_tokens(step)

    strip = 32

    @pl.loop(0, rows_t // strip)
    def _(step):
        rows = pl.ds(pl.multiple_of(step * strip, strip), strip)
        square = jnp.zeros((strip, 1), F32)
        for block in range(4):
            wide = tok[block, rows].astype(F32)
            square = square + jnp.sum(wide * wide, axis=1, keepdims=True)
        scale = lax.rsqrt(square / (4 * tok.shape[2]) + 1e-6)
        for block in range(4):
            gain = tok[block, pl.ds(rows_t, 16)][0:1].astype(F32)
            tok[block, rows] = (tok[block, rows].astype(F32) * scale * gain).astype(BF16)

    half = wq.shape[1] // 2
    width = qacc.shape[1]
    qacc[...] = jnp.zeros_like(qacc)

    def add_queries(owner, which):
        first = pl.multiple_of(which * half, half)

        @pl.loop(0, width // tile)
        def _(step):
            columns = pl.ds(pl.multiple_of(step * tile, tile), tile)
            qacc[:, columns] += jnp.dot(
                tok[owner, pl.ds(0, rows_t), pl.ds(first, half)],
                wq[owner, pl.ds(first, half), columns],
                preferred_element_type=F32,
            )

    own[3].wait()
    for which in range(2):
        add_queries(mine, which)
    q_panels.got_near()
    for which in range(2):
        add_queries(near, which)
    add_queries(far, group)
    for chunk in range(CHUNKS):
        q_panels.got_diagonal_far(chunk)
    add_queries(diagonal, group)
    q_panels.got_handed(1)
    out_panels.got_far(0)
    add_queries(far, 1 - group)
    for chunk in range(CHUNKS):
        q_panels.got_diagonal_handed(chunk)
    add_queries(diagonal, 1 - group)
    att[...] = qacc[...].astype(BF16)

    position = mine * rows_t + lax.broadcasted_iota(jnp.int32, (rows_t, 1), 0)
    placed = position.astype(F32)
    begun = (held_pos >= 0.0) & (held_pos <= placed)
    chosen = jnp.where(begun, 0, -1)
    chosen_pos = jnp.where(begun, held_pos, -1.0)
    for slot in range(slots):
        slot_pos = pos_ref[slot]
        eligible = (slot_pos >= 0) & (position >= slot_pos)
        chosen = jnp.where(eligible, slot + 1, chosen)
        chosen_pos = jnp.where(eligible, jnp.maximum(chosen_pos, slot_pos.astype(F32)), chosen_pos)
    doc_start = jnp.zeros((rows_t, 1), jnp.int32)
    start = jnp.int32(0)
    for doc in range(docs_ref.shape[0]):
        doc_start = jnp.where(position >= start, jnp.maximum(doc_start, start), doc_start)
        start = start + docs_ref[doc]
    opened = (chosen >= 0) & (chosen_pos >= doc_start.astype(F32))
    factor = jnp.where(opened, gate_ref[0], 0.0)
    keys = (slots + 1) * lat_rows
    image = lax.broadcasted_iota(jnp.int32, (rows_t, keys), 1) // lat_rows
    allowed = image == chosen

    @pl.loop(0, width // HEAD_DIM)
    def _(head):
        columns = pl.ds(pl.multiple_of(head * HEAD_DIM, HEAD_DIM), HEAD_DIM)
        shifted = pl.ds(pl.multiple_of(width + head * HEAD_DIM, HEAD_DIM), HEAD_DIM)
        scores = lax.dot_general(
            att[:, columns], kv[:, columns], (((1,), (1,)), ((), ())), preferred_element_type=F32
        )
        scores = jnp.where(allowed, scores * (1.0 / HEAD_DIM**0.5), -1e30)
        grown = jnp.exp(scores - jnp.max(scores, axis=1, keepdims=True))
        probs = (grown / jnp.sum(grown, axis=1, keepdims=True)).astype(BF16)
        att[:, columns] = jnp.dot(probs, kv[:, shifted], preferred_element_type=F32).astype(BF16)

    def up(block):
        return copy(SUM_UP + block, part.at[block], up_buf.at[block - 1], at(shard=z + 1))

    def down(block):
        return copy(SUM_DOWN + block, part.at[block], down_buf.at[block], at(shard=z - 1))

    def project(block):
        @pl.loop(0, wout.shape[2] // tile)
        def _(step):
            columns = pl.ds(pl.multiple_of(step * tile, tile), tile)
            part[block, :, columns] = jnp.dot(
                att[...], wout[block, :, columns], preferred_element_type=F32
            ).astype(BF16)

    def add(block, ref):
        @pl.loop(0, rows_t // strip)
        def _(step):
            rows = pl.ds(pl.multiple_of(step * strip, strip), strip)
            part[block, rows] = (part[block, rows].astype(F32) + ref[rows].astype(F32)).astype(BF16)

    def pass_on(block, edge):
        @pl.when((block > z) & ((z == 0) if edge else (z > 0)))
        def _():
            if not edge:
                up(block).wait_recv()
                add(block, up_buf.at[block - 1])
            up(block).start()

        @pl.when((block < z) & ((z == 3) if edge else (z < 3)))
        def _():
            if not edge:
                down(block).wait_recv()
                add(block, down_buf.at[block])
            down(block).start()

    order = (3 * x, x + 1, 3 - 3 * x, 2 - x)
    own[4].wait()
    out_panels.got_near()
    for block in order[:2]:
        project(block)
        pass_on(block, True)
    out_panels.got_far(1)
    out_panels.got_handed(0)
    for block in order[:1]:
        pass_on(block, False)
    out_panels.got_handed(1)
    for chunk in range(CHUNKS):
        out_panels.got_diagonal_far(chunk)
        out_panels.got_diagonal_handed(chunk)
    for block in order[2:]:
        project(block)
        pass_on(block, True)
    for block in order[1:]:
        pass_on(block, False)

    @pl.when(z > 0)
    def _():
        copy(SUM_UP + z, part.at[z], up_buf.at[z - 1], at(shard=z - 1)).wait_recv()
        add(z, up_buf.at[z - 1])

    @pl.when(z < 3)
    def _():
        copy(SUM_DOWN + z, part.at[z], down_buf.at[z], at(shard=z + 1)).wait_recv()
        add(z, down_buf.at[z])

    out_ref[...] = (tok_ref[...].astype(F32) + factor * part[z].astype(F32)).astype(BF16)

    for sending in carries:
        sending.wait_send()
    for panels in (kv_panels, q_panels, out_panels):
        panels.sent()
    for block in range(4):

        @pl.when(block > z)
        def _():
            up(block).wait_send()

        @pl.when(block < z)
        def _():
            down(block).wait_send()


def body(tokens, gain, w_query, w_key, w_value, w_out, latents, image_pos, doc_lengths, alpha):
    rows_t, features = tokens.shape
    slots = image_pos.shape[0]
    lat_rows = latents.shape[0] // slots
    heads_width, lat_width = w_query.shape[1], latents.shape[1]
    gain_rows = jnp.broadcast_to(gain[None, :], (16, features))
    tok_in = jnp.concatenate([tokens, gain_rows], axis=0)
    wkv = jnp.concatenate([w_key, w_value], axis=1)
    used = image_pos >= 0
    last_slot = jnp.maximum(jnp.max(jnp.where(used, jnp.arange(slots, dtype=jnp.int32), -1)), 0)
    last_pos = jnp.max(jnp.where(used, image_pos, -1))
    last_rows = lax.dynamic_slice_in_dim(latents, last_slot * lat_rows, lat_rows, 0)
    column = jnp.arange(lat_width, dtype=jnp.int32)[None, :]
    digits = jnp.where(column == 0, last_pos // 64, jnp.where(column == 1, last_pos % 64, 0))
    tag = jnp.broadcast_to(digits, (16, lat_width)).astype(BF16)
    carry_in = jnp.concatenate([last_rows, tag], axis=0)
    smem = pl.BlockSpec(memory_space=pltpu.SMEM)
    vmem = pl.BlockSpec(memory_space=pltpu.VMEM)
    anywhere = pl.BlockSpec(memory_space=pl.ANY)
    keys = (slots + 1) * lat_rows
    return pl.pallas_call(
        functools.partial(kernel, slots, lat_rows),
        out_shape=jax.ShapeDtypeStruct(tokens.shape, BF16),
        in_specs=[smem] * 3 + [anywhere, vmem] + [anywhere] * 4 + [vmem],
        out_specs=vmem,
        scratch_shapes=[
            pltpu.VMEM((4, rows_t + 16, features), BF16),
            pltpu.VMEM((4,) + w_query.shape, BF16),
            pltpu.VMEM((4,) + wkv.shape, BF16),
            pltpu.VMEM((4,) + w_out.shape, BF16),
            pltpu.VMEM((4,) + carry_in.shape, BF16),
            pltpu.VMEM((keys, lat_width), BF16),
            pltpu.VMEM((keys, 2 * heads_width), BF16),
            pltpu.VMEM((rows_t, heads_width), F32),
            pltpu.VMEM((rows_t, heads_width), BF16),
            pltpu.VMEM((4, rows_t, features), BF16),
            pltpu.VMEM((3, rows_t, features), BF16),
            pltpu.VMEM((3, rows_t, features), BF16),
            pltpu.SemaphoreType.DMA((TRANSFERS,)),
            pltpu.SemaphoreType.DMA((TRANSFERS,)),
            pltpu.SemaphoreType.DMA((5,)),
        ],
        compiler_params=pltpu.CompilerParams(
            collective_id=0, has_side_effects=True, vmem_limit_bytes=62 * 2**20
        ),
    )(
        image_pos,
        doc_lengths,
        jnp.tanh(alpha),
        tok_in,
        tokens,
        w_query,
        wkv,
        w_out,
        carry_in,
        latents,
    )


def solution(mesh):
    in_specs = (
        P(("groups", "ctx"), "shard"),
        P("shard"),
        P("ctx", "shard"),
        P("ctx", "shard"),
        P("ctx", "shard"),
        P("shard", "ctx"),
        P(("groups", "ctx"), None),
        P(("groups", "ctx")),
        P("groups"),
        P(),
    )
    out_specs = P(("groups", "ctx"), "shard")
    sizes = (mesh.shape["groups"], mesh.shape["ctx"], mesh.shape["shard"])
    chosen_body = body if sizes == (2, 4, 4) else plain_body
    return jax.shard_map(chosen_body, mesh=mesh, in_specs=in_specs, out_specs=out_specs, check_vma=False)
```
